32 devices in a mesh: morton: 16 (over z, y, x), chan: 2 (over core).
Axes of the slice: x: 2, y: 2, z: 4, core: 2. Of those that a mesh axis runs over, the one named last changes fastest.
Arguments:
- features: bfloat16 [128, 4, 4, 4, 256], P('morton', None, None, None, 'chan'), may hold values from -6 to 6
- weight: bfloat16 [27, 256, 256], replicated, may hold values from -0.078125 to 0.078125
- neighbours: int32 [128, 27], P('morton'), may hold values from 0 to 24, as said below
- send_slots: int32 [16, 2, 8], P('morton'), may hold values from 0 to 8, as said below
- grad_pooled: bfloat16 [128, 2, 2, 2, 256], P('morton', None, None, None, 'chan'), may hold values from -6 to 6
Outputs:
- pooled: bfloat16 [128, 2, 2, 2, 256], P('morton', None, None, None, 'chan')
- grad_features: bfloat16 [128, 4, 4, 4, 256], P('morton', None, None, None, 'chan')
- grad_weight: float32 [27, 256, 256], P(None, 'chan')
The draws below stay inside these ranges and needn't reach their ends.
Inputs may be any that keep to these rules, and one draw needn't show every extreme that they name: `neighbours`: entry k = 9 (a + 1) + 3 (e + 1) + (c + 1) of a block names the block at block offset (a, e, c), a along the first octant axis, encoded as in the first step. An offset with a = -1 names a block of the same device or an entry of the previous device's upward list, a = +1 one of the same device or of the next device's downward list, a = 0 one of the same device. The lists come from a grid of blocks: if block b names block c at offset o, block c names b at offset -o. Every occupied slot names itself at offset 13; an empty slot names no block at any offset, and no slot names an empty one or an unused list entry. send_slots[d, 0] lists the slots that device d sends to device d - 1, send_slots[d, 1] those it sends to device d + 1: distinct occupied slots first, then 8 for unused entries. Some device fills both of its lists in every draw. The first device's downward list and the last device's upward list are unused.
All inputs are finite; a program needn't handle non-finite values.
Results may differ from the reference program's by a relative error of at most 0.005.
Values may be sent and summed in bfloat16 or wider, within the bound.
A program may use at most 128 MiB of HBM per device.

```python
import jax
import jax.numpy as jnp
from jax import lax

CHANNELS = 256
SPAN_X = 1
CROSS_Y = 4
CROSS_Z = 2
BLOCKS_DEV = 8
SLOTS = 8
BLOCKS = 128
N_MORTON = 16


def plane_list(plane_live, plane_slot):
    count_dev = plane_live.shape[0]
    markers = plane_live.reshape(count_dev, -1).astype(jnp.int32)
    before = jnp.cumsum(markers, axis=1) - markers
    target = jnp.where(markers > 0, before, SLOTS)
    listing = jnp.full((count_dev, SLOTS), BLOCKS_DEV, jnp.int32)
    device_rows = jnp.broadcast_to(jnp.arange(count_dev, dtype=jnp.int32)[:, None], target.shape)
    listing = listing.at[device_rows, target].set(plane_slot.reshape(count_dev, -1).astype(jnp.int32), mode='drop')
    return (listing, before.reshape(plane_live.shape))


def geometry(key):
    folded = jax.random.fold_in(key, 11)
    key_rate, key_full, key_toss, key_order = jax.random.split(folded, 4)
    count_dev = N_MORTON
    percent = jax.random.randint(key_rate, (count_dev,), 45, 101)
    busiest = jax.random.randint(key_full, (), 1, count_dev - 1)
    tosses = jax.random.randint(key_toss, (count_dev, SPAN_X, CROSS_Y, CROSS_Z), 0, 100)
    device_ids = jnp.arange(count_dev, dtype=jnp.int32)
    forced = jnp.abs(device_ids - busiest) <= 1
    occupied = (tosses < percent[:, None, None, None]) | forced[:, None, None, None]
    cell_of_slot = jax.vmap(lambda sub_key: jax.random.permutation(sub_key, BLOCKS_DEV))(jax.random.split(key_order, count_dev)).astype(jnp.int32)
    slot_of_cell = jnp.argsort(cell_of_slot, axis=1).astype(jnp.int32)
    slot_grid = slot_of_cell.reshape(count_dev, SPAN_X, CROSS_Y, CROSS_Z)
    down_list, down_place = plane_list(occupied[:, 0], slot_grid[:, 0])
    up_list, up_place = plane_list(occupied[:, SPAN_X - 1], slot_grid[:, SPAN_X - 1])
    down_list = jnp.where(device_ids[:, None] == 0, BLOCKS_DEV, down_list)
    up_list = jnp.where(device_ids[:, None] == count_dev - 1, BLOCKS_DEV, up_list)
    outgoing = jnp.stack([down_list, up_list], axis=1).astype(jnp.int32)
    lower_live = jnp.roll(occupied[:, SPAN_X - 1], 1, axis=0) & (device_ids >= 1)[:, None, None]
    lower_place = jnp.roll(up_place, 1, axis=0)
    upper_live = jnp.roll(occupied[:, 0], -1, axis=0) & (device_ids <= count_dev - 2)[:, None, None]
    upper_place = jnp.roll(down_place, -1, axis=0)
    shape_grid = (SPAN_X, CROSS_Y, CROSS_Z)
    pos_x = lax.broadcasted_iota(jnp.int32, shape_grid, 0)
    pos_y = lax.broadcasted_iota(jnp.int32, shape_grid, 1)
    pos_z = lax.broadcasted_iota(jnp.int32, shape_grid, 2)
    entries = []
    for a in (-1, 0, 1):
        for e in (-1, 0, 1):
            for c in (-1, 0, 1):
                near_x = pos_x + a
                near_y = pos_y + e
                near_z = pos_z + c
                inside = (near_y >= 0) & (near_y < CROSS_Y) & (near_z >= 0) & (near_z < CROSS_Z)
                clip_x = jnp.clip(near_x, 0, SPAN_X - 1)
                clip_y = jnp.clip(near_y, 0, CROSS_Y - 1)
                clip_z = jnp.clip(near_z, 0, CROSS_Z - 1)
                own_code = jnp.where(occupied[:, clip_x, clip_y, clip_z], slot_grid[:, clip_x, clip_y, clip_z], BLOCKS_DEV)
                low_code = jnp.where(lower_live[:, clip_y, clip_z], BLOCKS_DEV + 1 + lower_place[:, clip_y, clip_z], BLOCKS_DEV)
                high_code = jnp.where(upper_live[:, clip_y, clip_z], BLOCKS_DEV + 1 + SLOTS + upper_place[:, clip_y, clip_z], BLOCKS_DEV)
                encoded = jnp.where(near_x < 0, low_code, jnp.where(near_x >= SPAN_X, high_code, own_code))
                encoded = jnp.where(inside[None] & occupied, encoded, BLOCKS_DEV)
                entries.append(encoded)
    lookup = jnp.stack(entries, axis=-1).reshape(count_dev, BLOCKS_DEV, 27)
    ordered = jnp.take_along_axis(lookup, cell_of_slot[:, :, None], axis=1)
    return (ordered.reshape(count_dev * BLOCKS_DEV, 27).astype(jnp.int32), outgoing)


def draw_neighbours(key, part):
    return geometry(key)[0]


def draw_send_slots(key, part):
    return geometry(key)[1]


def block_scale(rng, extent, cuts, low, high):
    def one(dim, shards_of):
        draws = jax.random.uniform(jax.random.fold_in(jax.random.fold_in(rng, 6), dim), (shards_of,), jnp.float32, low / len(cuts), high / len(cuts))
        return jnp.repeat(jnp.exp(draws), extent[dim] // shards_of).reshape((-1,) + (1,) * (len(extent) - dim - 1))

    factor_of = one(*cuts[0])
    for cut in cuts[1:]:
        factor_of = factor_of * one(*cut)
    return factor_of


def gaussian(key, dims, scale, most, cuts=(), kind=jnp.bfloat16):
    loudness = block_scale(key, dims, cuts, -0.22, 0.18) if cuts else 1.0
    array = jax.random.normal(key, dims, jnp.float32) * scale * loudness
    return jnp.minimum(jnp.maximum(array, -most), most).astype(kind)


def setup_inputs(seed: int = 0) -> dict:
    streams_of = jax.random.split(jax.random.key(seed), 6)
    return {
        "features": gaussian(streams_of[0], (BLOCKS, 4, 4, 4, CHANNELS), 1.0, 6.0, ((0, 16), (4, 2))),
        "weight": gaussian(streams_of[1], (27, CHANNELS, CHANNELS), (27 * CHANNELS) ** -0.5, 0.078125),
        "neighbours": draw_neighbours(jax.random.fold_in(streams_of[5], 71), 0),
        "send_slots": draw_send_slots(jax.random.fold_in(streams_of[5], 71), 0),
        "grad_pooled": gaussian(streams_of[4], (BLOCKS, 2, 2, 2, CHANNELS), 1.0, 6.0, ((0, 16), (4, 2))),
    }


def build_tile(extended, lookup):
    layers = ((3, 4), (0, 4), (0, 1))
    planes = []
    for a in range(3):
        strips = []
        for e in range(3):
            columns = []
            for c in range(3):
                source = extended[:, layers[a][0]:layers[a][1], layers[e][0]:layers[e][1], layers[c][0]:layers[c][1], :]
                portion = jnp.take(source, lookup[:, 9 * a + 3 * e + c], axis=0)
                columns.append(portion)
            strips.append(jnp.concatenate(columns, axis=3))
        planes.append(jnp.concatenate(strips, axis=2))
    return jnp.concatenate(planes, axis=1)

def convolve(octant_tile, kernel):
    blocks = octant_tile.shape[0]
    summed = None
    for a in range(3):
        for e in range(3):
            for c in range(3):
                window = octant_tile[:, a:a + 4, e:e + 4, c:c + 4, :].reshape(blocks * 64, octant_tile.shape[-1])
                product = jnp.dot(window, kernel[9 * a + 3 * e + c], precision=lax.Precision.HIGHEST, preferred_element_type=jnp.float32)
                summed = product if summed is None else summed + product
    return summed

def global_index(neighbours, send_slots):
    row_ids = jnp.arange(BLOCKS, dtype=jnp.int32)[:, None]
    device_of = row_ids // BLOCKS_DEV
    flat_slots = send_slots.reshape(-1)
    lower_dev = jnp.maximum(device_of - 1, 0)
    upper_dev = jnp.minimum(device_of + 1, N_MORTON - 1)
    lower_pos = jnp.clip(neighbours - BLOCKS_DEV - 1, 0, SLOTS - 1)
    upper_pos = jnp.clip(neighbours - BLOCKS_DEV - 1 - SLOTS, 0, SLOTS - 1)
    lower_slot = flat_slots[lower_dev * 2 * SLOTS + SLOTS + lower_pos]
    upper_slot = flat_slots[upper_dev * 2 * SLOTS + upper_pos]
    lower_row = jnp.where(lower_slot == BLOCKS_DEV, BLOCKS, lower_dev * BLOCKS_DEV + lower_slot)
    upper_row = jnp.where(upper_slot == BLOCKS_DEV, BLOCKS, upper_dev * BLOCKS_DEV + upper_slot)
    own_row = device_of * BLOCKS_DEV + neighbours
    picked = jnp.where(neighbours <= BLOCKS_DEV + SLOTS, lower_row, upper_row)
    picked = jnp.where(neighbours == BLOCKS_DEV, BLOCKS, picked)
    picked = jnp.where(neighbours < BLOCKS_DEV, own_row, picked)
    return picked.astype(jnp.int32)

def reference(features, weight, neighbours, send_slots, grad_pooled):
    lookup = global_index(neighbours, send_slots)
    groups = lookup.reshape(N_MORTON, BLOCKS_DEV, 27)

    def forward(feature_vals, kernel):
        extended = jnp.concatenate([feature_vals, jnp.zeros((1, 4, 4, 4, CHANNELS), jnp.float32)], axis=0)

        def one_group(group_rows):
            return convolve(build_tile(extended, group_rows), kernel)
        return lax.map(one_group, groups).reshape(BLOCKS, 4, 4, 4, CHANNELS)
    conv_out, pullback = jax.vjp(forward, features.astype(jnp.float32), weight.astype(jnp.float32))
    squashed = jax.nn.sigmoid(conv_out)
    activated = conv_out * squashed
    pooled = activated.reshape(BLOCKS, 2, 2, 2, 2, 2, 2, CHANNELS).mean(axis=(2, 4, 6)).astype(jnp.bfloat16)
    scaled = grad_pooled.astype(jnp.float32) / 8.0
    spread = jnp.broadcast_to(scaled[:, :, None, :, None, :, None, :], (BLOCKS, 2, 2, 2, 2, 2, 2, CHANNELS)).reshape(BLOCKS, 4, 4, 4, CHANNELS)
    grad_pre = (spread * squashed * (1.0 + conv_out * (1.0 - squashed))).astype(jnp.bfloat16)
    cotangent = lax.optimization_barrier(grad_pre).astype(jnp.float32)
    grad_inputs, grad_kernel = pullback(cotangent)
    return (pooled, grad_inputs.astype(jnp.bfloat16), grad_kernel)
```

```python
import functools

import jax
import jax.numpy as jnp
from jax import lax
from jax.experimental import pallas as pl
from jax.experimental.pallas import tpu as pltpu
from jax.sharding import PartitionSpec as P

MESH = pl.DeviceIdType.MESH
F32 = jnp.float32
BF16 = jnp.bfloat16


def offsets_of(x):
    return ([-1] if x == 3 else []) + [0] + ([1] if x == 0 else [])


def place(offset, x):
    return 0 if offset < 0 else (5 if offset > 0 else x + 1)


def rim_copies(own, low, high, send, recv, me, core, n):
    nxt, prv = lax.rem(me + 1, n), lax.rem(me + n - 1, n)
    rows = own.shape[1]
    plane = rows // 4
    peer = 1 - core
    copies = [
        pltpu.make_async_remote_copy(
            src_ref=own.at[core], dst_ref=own.at[core], send_sem=send.at[0],
            recv_sem=recv.at[0], device_id=(me, peer), device_id_type=MESH,
        )
    ]
    for target in range(2):
        copies.append(
            pltpu.make_async_remote_copy(
                src_ref=own.at[core, pl.ds(rows - plane, plane)], dst_ref=low.at[core],
                send_sem=send.at[1 + target], recv_sem=recv.at[1 + core],
                device_id=(nxt, target), device_id_type=MESH,
            )
        )
        copies.append(
            pltpu.make_async_remote_copy(
                src_ref=own.at[core, pl.ds(0, plane)], dst_ref=high.at[core],
                send_sem=send.at[3 + target], recv_sem=recv.at[3 + core],
                device_id=(prv, target), device_id_type=MESH,
            )
        )
    return copies


def wait_peer(own, send, recv, me, core):
    pltpu.make_async_remote_copy(
        src_ref=own.at[1 - core], dst_ref=own.at[1 - core], send_sem=send.at[0],
        recv_sem=recv.at[0], device_id=(me, 1 - core), device_id_type=MESH,
    ).wait_recv()


def wait_rims(own, low, high, send, recv, me, core):
    for half in range(2):
        for ref, base in ((low, 1), (high, 3)):
            pltpu.make_async_remote_copy(
                src_ref=ref.at[half], dst_ref=ref.at[half], send_sem=send.at[0],
                recv_sem=recv.at[base + half], device_id=(me, 1 - core), device_id_type=MESH,
            ).wait_recv()


def fill_interior(tile, own, occ, half, blocks):
    value = own[half].astype(F32).reshape(4, 4, 4, blocks, own.shape[-1])
    tile[half, 1:5, 1:5, 1:5] = value * occ


def fill_border(tile, low, high, pick, blocks):
    width = low.shape[-1]
    for x in range(4):
        for y in range(4):
            for z in range(4):
                ks = [
                    (a, e, c)
                    for a in offsets_of(x)
                    for e in offsets_of(y)
                    for c in offsets_of(z)
                    if (a, e, c) != (0, 0, 0)
                ]
                if not ks:
                    continue
                left = jnp.concatenate(
                    [pick[9 * a + 3 * e + c + 13] for a, e, c in ks], axis=0
                )
                own = jnp.concatenate([tile[h, 1 + x, 1 + y, 1 + z] for h in range(2)], axis=1)
                if x in (0, 3):
                    rim = high if x == 0 else low
                    r = (4 * y + z) * blocks
                    other = jnp.concatenate(
                        [rim[h, r : r + blocks, :].astype(F32) for h in range(2)], axis=1
                    )
                    right = jnp.concatenate([own, other], axis=0)
                else:
                    right = own
                got = jnp.dot(
                    left[:, : right.shape[0]].astype(BF16), right.astype(BF16),
                    preferred_element_type=F32,
                )
                for j, (a, e, c) in enumerate(ks):
                    for h in range(2):
                        tile[h, place(a, x), place(e, y), place(c, z)] = got[
                            j * blocks : (j + 1) * blocks, h * width : (h + 1) * width
                        ]


def window(tile, half, a, e, c):
    part = tile[half, a : a + 4, e : e + 4, c : c + 4]
    return part.reshape(-1, part.shape[-1]).astype(BF16)


def kernel(
    n, feat_ref, weight_ref, names_ref, occ_ref, sel_ref, gp_ref,
    pooled_ref, gf_ref, gw_ref,
    wf, wb, feat, flow, fhigh, grad, glow, ghigh, tile_in, tile_g, pick, merge,
    stage, pool_stage, wsem, fsend, frecv, gsend, grecv, ssend, srecv,
):
    me, core = lax.axis_index("morton"), lax.axis_index("chan")
    nxt, prv = lax.rem(me + 1, n), lax.rem(me + n - 1, n)
    width = feat_ref.shape[-1]
    rows = feat_ref.shape[0]
    blocks = rows // 64
    columns = pl.ds(pl.multiple_of(core * width, width), width)
    load_f = pltpu.make_async_copy(weight_ref.at[:, :, columns], wf, wsem.at[0])
    load_b = pltpu.make_async_copy(weight_ref.at[:, columns, :], wb, wsem.at[1])
    load_f.start()
    load_b.start()
    barrier = pltpu.get_barrier_semaphore()
    for target in ((me, 1 - core), (nxt, 0), (nxt, 1), (prv, 0), (prv, 1)):
        pl.semaphore_signal(barrier, inc=1, device_id=target, device_id_type=MESH)
    stage[...] = feat_ref[...].astype(F32)
    feat[core] = jnp.concatenate(
        [stage[pl.ds(p, blocks, stride=64), :] for p in range(64)], axis=0
    ).astype(BF16)
    pl.semaphore_wait(barrier, 5)
    sels = [
        pltpu.make_async_remote_copy(
            src_ref=sel_ref.at[1], dst_ref=merge.at[0], send_sem=ssend.at[0],
            recv_sem=srecv.at[0], device_id=(nxt, core), device_id_type=MESH,
        ),
        pltpu.make_async_remote_copy(
            src_ref=sel_ref.at[0], dst_ref=merge.at[1], send_sem=ssend.at[1],
            recv_sem=srecv.at[1], device_id=(prv, core), device_id_type=MESH,
        ),
    ]
    copies = rim_copies(feat, flow, fhigh, fsend, frecv, me, core, n)
    for copy in sels + copies:
        copy.start()
    occ = occ_ref[...]
    fill_interior(tile_in, feat, occ, core, blocks)
    for copy in sels:
        copy.wait()
    eye = (
        lax.broadcasted_iota(jnp.int32, (blocks, width), 0)
        == lax.broadcasted_iota(jnp.int32, (blocks, width), 1)
    ).astype(F32)
    pick[0:9] = jnp.dot(
        names_ref[0:9].reshape(9 * blocks, width)[:, : 2 * blocks],
        jnp.concatenate([eye, merge[0]], axis=0), preferred_element_type=F32,
    ).reshape(9, blocks, width)
    pick[9:18] = names_ref[9:18]
    pick[18:27] = jnp.dot(
        names_ref[18:27].reshape(9 * blocks, width)[:, : 2 * blocks],
        jnp.concatenate([eye, merge[1]], axis=0), preferred_element_type=F32,
    ).reshape(9, blocks, width)
    wait_peer(feat, fsend, frecv, me, core)
    fill_interior(tile_in, feat, occ, 1 - core, blocks)
    wait_rims(feat, flow, fhigh, fsend, frecv, me, core)
    fill_border(tile_in, flow, fhigh, pick, blocks)
    load_f.wait()
    acc = None
    for a in range(3):
        for e in range(3):
            left = jnp.concatenate(
                [window(tile_in, h, a, e, c) for c in range(3) for h in range(2)], axis=1
            )
            k = 9 * a + 3 * e
            right = wf[k : k + 3].reshape(6 * width, width)
            term = jnp.dot(left, right, preferred_element_type=F32)
            acc = term if acc is None else acc + term
    s = jax.nn.sigmoid(acc)
    act = (acc * s).reshape(2, 2, 2, 2, 2, 2, blocks, width)
    summed = act[:, 0] + act[:, 1]
    summed = summed[:, :, 0] + summed[:, :, 1]
    summed = summed[:, :, :, 0] + summed[:, :, :, 1]
    slope = (s * (1.0 + acc * (1.0 - s))).reshape(2, 2, 2, 2, 2, 2, blocks, width)
    pool_stage[0] = gp_ref[...].astype(F32) * 0.125
    for x in range(2):
        for y in range(2):
            for z in range(2):
                q = 4 * x + 2 * y + z
                g = pool_stage[0, pl.ds(q, blocks, stride=8), :]
                pool_stage[1, pl.ds(q, blocks, stride=8), :] = summed[x, y, z] * 0.125
                for i in range(2):
                    for j in range(2):
                        for l in range(2):
                            p = 16 * (2 * x + i) + 4 * (2 * y + j) + 2 * z + l
                            stage[p * blocks : (p + 1) * blocks, :] = g * slope[x, i, y, j, z, l]
    grad[core] = stage[...].astype(BF16)
    pooled_ref[...] = pool_stage[1].astype(BF16)
    gcopies = rim_copies(grad, glow, ghigh, gsend, grecv, me, core, n)
    for copy in gcopies:
        copy.start()
    fill_interior(tile_g, grad, occ, core, blocks)
    wait_peer(grad, gsend, grecv, me, core)
    fill_interior(tile_g, grad, occ, 1 - core, blocks)
    flipped = jnp.concatenate([grad[0], grad[1]], axis=1).T
    for k in range(27):
        gw_ref[k] = jnp.dot(
            flipped, window(tile_in, core, k // 9, k // 3 % 3, k % 3), preferred_element_type=F32
        )
    wait_rims(grad, glow, ghigh, gsend, grecv, me, core)
    fill_border(tile_g, glow, ghigh, pick, blocks)
    load_b.wait()
    acc = None
    for a in range(3):
        for e in range(3):
            left = jnp.concatenate(
                [window(tile_g, h, 2 - a, 2 - e, 2 - c) for c in range(3) for h in range(2)],
                axis=1,
            )
            k = 9 * a + 3 * e
            right = jnp.concatenate([wb[k + c] for c in range(3)], axis=1)
            term = lax.dot_general(
                left, right, (((1,), (1,)), ((), ())), preferred_element_type=F32
            )
            acc = term if acc is None else acc + term
    for p in range(64):
        stage[pl.ds(p, blocks, stride=64), :] = acc[p * blocks : (p + 1) * blocks]
    gf_ref[...] = stage[...].astype(BF16)
    for copy in copies + gcopies:
        copy.wait_send()


def body(features, weight, neighbours, send_slots, grad_pooled):
    n = lax.axis_size("morton")
    blocks = features.shape[0]
    width = features.shape[-1]
    full = weight.shape[-1]
    slots = send_slots.shape[-1]
    lanes = jnp.arange(width, dtype=jnp.int32)
    column = jnp.where(neighbours > blocks, neighbours - 1, neighbours)
    column = jnp.where(neighbours > blocks + slots, column - slots, column)
    column = jnp.where(neighbours == blocks, -1, column)
    names = (column.T[:, :, None] == lanes).astype(F32)
    occ = jnp.broadcast_to((neighbours[:, 13] < blocks).astype(F32)[:, None], (blocks, width))
    places = jnp.where(send_slots[0] < blocks, send_slots[0] + blocks, -1)
    sel = (places[:, :, None] == lanes).astype(F32)
    rows = blocks * 64
    vmem = pl.BlockSpec(memory_space=pltpu.VMEM)
    pooled, gf, gw = pl.pallas_call(
        functools.partial(kernel, n),
        out_shape=(
            jax.ShapeDtypeStruct((blocks * 8, width), BF16),
            jax.ShapeDtypeStruct((rows, width), BF16),
            jax.ShapeDtypeStruct((27, full, width), F32),
        ),
        in_specs=[vmem, pl.BlockSpec(memory_space=pl.ANY), vmem, vmem, vmem, vmem],
        out_specs=(vmem, vmem, vmem),
        scratch_shapes=[
            pltpu.VMEM((27, full, width), BF16),
            pltpu.VMEM((27, width, full), BF16),
            pltpu.VMEM((2, rows, width), BF16),
            pltpu.VMEM((2, rows // 4, width), BF16),
            pltpu.VMEM((2, rows // 4, width), BF16),
            pltpu.VMEM((2, rows, width), BF16),
            pltpu.VMEM((2, rows // 4, width), BF16),
            pltpu.VMEM((2, rows // 4, width), BF16),
            pltpu.VMEM((2, 6, 6, 6, blocks, width), F32),
            pltpu.VMEM((2, 6, 6, 6, blocks, width), F32),
            pltpu.VMEM((27, blocks, width), F32),
            pltpu.VMEM((2, slots, width), F32),
            pltpu.VMEM((rows, width), F32),
            pltpu.VMEM((2, blocks * 8, width), F32),
            pltpu.SemaphoreType.DMA((2,)),
            pltpu.SemaphoreType.DMA((5,)),
            pltpu.SemaphoreType.DMA((5,)),
            pltpu.SemaphoreType.DMA((5,)),
            pltpu.SemaphoreType.DMA((5,)),
            pltpu.SemaphoreType.DMA((2,)),
            pltpu.SemaphoreType.DMA((2,)),
        ],
        compiler_params=pltpu.CompilerParams(
            collective_id=0, has_side_effects=True, vmem_limit_bytes=48 * 1024 * 1024
        ),
    )(
        features.reshape(rows, width), weight, names, occ, sel,
        grad_pooled.reshape(blocks * 8, width),
    )
    gw = lax.psum(gw, "morton")
    return (
        pooled.reshape(grad_pooled.shape),
        gf.reshape(features.shape),
        jnp.swapaxes(gw, 1, 2),
    )


def solution(mesh):
    in_specs = (
        P("morton", None, None, None, "chan"),
        P(),
        P("morton", None),
        P("morton", None, None),
        P("morton", None, None, None, "chan"),
    )
    out_specs = (
        P("morton", None, None, None, "chan"),
        P("morton", None, None, None, "chan"),
        P(None, "chan", None),
    )
    return jax.shard_map(body, mesh=mesh, in_specs=in_specs, out_specs=out_specs, check_vma=False)
```

```python
import functools

import jax
import jax.numpy as jnp
from jax import lax
from jax.experimental import pallas as pl
from jax.experimental.pallas import tpu as pltpu
from jax.sharding import PartitionSpec as P

MESH = pl.DeviceIdType.MESH
F32 = jnp.float32
BF16 = jnp.bfloat16


def offsets_of(x):
    return ([-1] if x == 3 else []) + [0] + ([1] if x == 0 else [])


def place(offset, x):
    return 0 if offset < 0 else (5 if offset > 0 else x + 1)


def rim_copies(own, low, high, send, recv, me, core, n):
    nxt, prv = lax.rem(me + 1, n), lax.rem(me + n - 1, n)
    rows = own.shape[1]
    plane = rows // 4
    peer = 1 - core
    copies = [
        pltpu.make_async_remote_copy(
            src_ref=own.at[core], dst_ref=own.at[core], send_sem=send.at[0],
            recv_sem=recv.at[0], device_id=(me, peer), device_id_type=MESH,
        )
    ]
    for target in range(2):
        copies.append(
            pltpu.make_async_remote_copy(
                src_ref=own.at[core, pl.ds(rows - plane, plane)], dst_ref=low.at[core],
                send_sem=send.at[1 + target], recv_sem=recv.at[1 + core],
                device_id=(nxt, target), device_id_type=MESH,
            )
        )
        copies.append(
            pltpu.make_async_remote_copy(
                src_ref=own.at[core, pl.ds(0, plane)], dst_ref=high.at[core],
                send_sem=send.at[3 + target], recv_sem=recv.at[3 + core],
                device_id=(prv, target), device_id_type=MESH,
            )
        )
    return copies


def wait_peer(own, send, recv, me, core):
    pltpu.make_async_remote_copy(
        src_ref=own.at[1 - core], dst_ref=own.at[1 - core], send_sem=send.at[0],
        recv_sem=recv.at[0], device_id=(me, 1 - core), device_id_type=MESH,
    ).wait_recv()


def wait_rims(own, low, high, send, recv, me, core):
    for half in range(2):
        for ref, base in ((low, 1), (high, 3)):
            pltpu.make_async_remote_copy(
                src_ref=ref.at[half], dst_ref=ref.at[half], send_sem=send.at[0],
                recv_sem=recv.at[base + half], device_id=(me, 1 - core), device_id_type=MESH,
            ).wait_recv()


def fill_interior(tile, own, occ, half, blocks):
    value = own[half].astype(F32).reshape(4, 4, 4, blocks, own.shape[-1])
    tile[half, 1:5, 1:5, 1:5] = value * occ


def fill_border(tile, low, high, pick, blocks):
    width = low.shape[-1]
    for x in range(4):
        for y in range(4):
            for z in range(4):
                ks = [
                    (a, e, c)
                    for a in offsets_of(x)
                    for e in offsets_of(y)
                    for c in offsets_of(z)
                    if (a, e, c) != (0, 0, 0)
                ]
                if not ks:
                    continue
                left = jnp.concatenate(
                    [pick[9 * a + 3 * e + c + 13] for a, e, c in ks], axis=0
                )
                own = jnp.concatenate([tile[h, 1 + x, 1 + y, 1 + z] for h in range(2)], axis=1)
                if x in (0, 3):
                    rim = high if x == 0 else low
                    r = (4 * y + z) * blocks
                    other = jnp.concatenate(
                        [rim[h, r : r + blocks, :].astype(F32) for h in range(2)], axis=1
                    )
                    right = jnp.concatenate([own, other], axis=0)
                else:
                    right = own
                got = jnp.dot(
                    left[:, : right.shape[0]].astype(BF16), right.astype(BF16),
                    preferred_element_type=F32,
                )
                for j, (a, e, c) in enumerate(ks):
                    for h in range(2):
                        tile[h, place(a, x), place(e, y), place(c, z)] = got[
                            j * blocks : (j + 1) * blocks, h * width : (h + 1) * width
                        ]


def window(tile, half, a, e, c):
    part = tile[half, a : a + 4, e : e + 4, c : c + 4]
    return part.reshape(-1, part.shape[-1]).astype(BF16)


CUTS = (0, 7, 14, 21, 27)


def bit_orders(n):
    bits = []
    while 2 ** len(bits) < n:
        bits.append(2 ** len(bits))
    swapped = bits[1::-1] + bits[2:]
    return (bits, swapped)


class Summing:
    def __init__(self, piece, n, me, core, acc, out, sends, recvs, sem):
        self.k0, self.k1 = CUTS[piece], CUTS[piece + 1]
        self.piece, self.me, self.core = piece, me, core
        self.acc, self.out, self.sends, self.recvs = acc, out, sends, recvs
        self.sem = sem
        self.bits = bit_orders(n)[piece % 2]
        self.low, self.size = 0, acc.shape[1]
        self.trail, self.pending = [], None

    def partner(self, bit):
        mine = lax.rem(lax.div(self.me, bit), 2)
        return mine, self.me + bit * (1 - 2 * mine)

    def rows(self, low, size):
        if isinstance(low, int):
            return pl.ds(low, size)
        return pl.ds(pl.multiple_of(low, 16), size)

    def copy(self, step, src, dst, to):
        pair = self.sem.at[self.piece, step]
        return pltpu.make_async_remote_copy(
            src_ref=src, dst_ref=dst, send_sem=pair.at[0], recv_sem=pair.at[1],
            device_id=(to, self.core), device_id_type=MESH,
        )

    def start_sum(self, step):
        ks = pl.ds(self.k0, self.k1 - self.k0)
        mine, to = self.partner(self.bits[step])
        halves = self.size > 16
        part = self.size // 2 if halves else self.size
        gone = self.low + (1 - mine) * part if halves else self.low
        kept = self.low + mine * part if halves else self.low
        send = self.sends[step].at[ks]
        send[...] = self.acc[ks, self.rows(gone, part), :].astype(BF16)
        copy = self.copy(step, send, self.recvs[step].at[ks], to)
        copy.start()
        self.pending = copy
        self.trail.append((self.bits[step], halves, self.low, self.size))
        self.low, self.size = kept, part

    def end_sum(self, step):
        ks = pl.ds(self.k0, self.k1 - self.k0)
        self.pending.wait()
        rows = self.rows(self.low, self.size)
        own = self.acc[ks, rows, :]
        if not self.trail[-1][1]:
            own = self.sends[step][ks].astype(F32)
        total = own + self.recvs[step][ks].astype(F32)
        if step + 1 < len(self.bits):
            self.acc[ks, rows, :] = total
        else:
            self.out[ks, rows, :] = total.astype(BF16)
            self.trail = [t for t in self.trail if t[1]]

    def start_gather(self, step):
        bit, _, low, size = self.trail[-1 - step]
        ks = pl.ds(self.k0, self.k1 - self.k0)
        _, to = self.partner(bit)
        held = self.out.at[ks, self.rows(self.low, self.size)]
        copy = self.copy(len(self.bits) + step, held, held, to)
        copy.start()
        self.pending = copy
        self.low, self.size = low, size

    def end_gather(self):
        self.pending.wait()


def kernel(
    n, feat_ref, weight_ref, names_ref, occ_ref, sel_ref, gp_ref,
    pooled_ref, gf_ref, gw_ref,
    wf, wb, feat, flow, fhigh, grad, glow, ghigh, tile_in, tile_g, pick, merge,
    stage, pool_stage, wsem, fsend, frecv, gsend, grecv, ssend, srecv, total, rsem, *bufs,
):
    me, core = lax.axis_index("morton"), lax.axis_index("chan")
    nxt, prv = lax.rem(me + 1, n), lax.rem(me + n - 1, n)
    width = feat_ref.shape[-1]
    rows = feat_ref.shape[0]
    blocks = rows // 64
    columns = pl.ds(pl.multiple_of(core * width, width), width)
    load_f = pltpu.make_async_copy(weight_ref.at[:, :, columns], wf, wsem.at[0])
    load_b = pltpu.make_async_copy(weight_ref.at[:, columns, :], wb, wsem.at[1])
    load_f.start()
    load_b.start()
    barrier = pltpu.get_barrier_semaphore()
    steps = len(bufs) // 2
    sums = [
        Summing(i, n, me, core, total, gw_ref, bufs[:steps], bufs[steps:], rsem)
        for i in range(len(CUTS) - 1)
    ]
    others = [(sums[0].partner(bit)[1], core) for bit in sums[0].bits]
    for target in [(me, 1 - core), (nxt, 0), (nxt, 1), (prv, 0), (prv, 1)] + others:
        pl.semaphore_signal(barrier, inc=1, device_id=target, device_id_type=MESH)
    stage[...] = feat_ref[...].astype(F32)
    feat[core] = jnp.concatenate(
        [stage[pl.ds(p, blocks, stride=64), :] for p in range(64)], axis=0
    ).astype(BF16)
    pl.semaphore_wait(barrier, 5 + len(others))
    sels = [
        pltpu.make_async_remote_copy(
            src_ref=sel_ref.at[1], dst_ref=merge.at[0], send_sem=ssend.at[0],
            recv_sem=srecv.at[0], device_id=(nxt, core), device_id_type=MESH,
        ),
        pltpu.make_async_remote_copy(
            src_ref=sel_ref.at[0], dst_ref=merge.at[1], send_sem=ssend.at[1],
            recv_sem=srecv.at[1], device_id=(prv, core), device_id_type=MESH,
        ),
    ]
    copies = rim_copies(feat, flow, fhigh, fsend, frecv, me, core, n)
    for copy in sels + copies:
        copy.start()
    occ = occ_ref[...]
    fill_interior(tile_in, feat, occ, core, blocks)
    for copy in sels:
        copy.wait()
    eye = (
        lax.broadcasted_iota(jnp.int32, (blocks, width), 0)
        == lax.broadcasted_iota(jnp.int32, (blocks, width), 1)
    ).astype(F32)
    pick[0:9] = jnp.dot(
        names_ref[0:9].reshape(9 * blocks, width)[:, : 2 * blocks],
        jnp.concatenate([eye, merge[0]], axis=0), preferred_element_type=F32,
    ).reshape(9, blocks, width)
    pick[9:18] = names_ref[9:18]
    pick[18:27] = jnp.dot(
        names_ref[18:27].reshape(9 * blocks, width)[:, : 2 * blocks],
        jnp.concatenate([eye, merge[1]], axis=0), preferred_element_type=F32,
    ).reshape(9, blocks, width)
    wait_peer(feat, fsend, frecv, me, core)
    fill_interior(tile_in, feat, occ, 1 - core, blocks)
    wait_rims(feat, flow, fhigh, fsend, frecv, me, core)
    fill_border(tile_in, flow, fhigh, pick, blocks)
    load_f.wait()
    acc = None
    for a in range(3):
        for e in range(3):
            left = jnp.concatenate(
                [window(tile_in, h, a, e, c) for c in range(3) for h in range(2)], axis=1
            )
            k = 9 * a + 3 * e
            right = wf[k : k + 3].reshape(6 * width, width)
            term = jnp.dot(left, right, preferred_element_type=F32)
            acc = term if acc is None else acc + term
    s = jax.nn.sigmoid(acc)
    act = (acc * s).reshape(2, 2, 2, 2, 2, 2, blocks, width)
    summed = act[:, 0] + act[:, 1]
    summed = summed[:, :, 0] + summed[:, :, 1]
    summed = summed[:, :, :, 0] + summed[:, :, :, 1]
    slope = (s * (1.0 + acc * (1.0 - s))).reshape(2, 2, 2, 2, 2, 2, blocks, width)
    pool_stage[0] = gp_ref[...].astype(F32) * 0.125
    for x in range(2):
        for y in range(2):
            for z in range(2):
                q = 4 * x + 2 * y + z
                g = pool_stage[0, pl.ds(q, blocks, stride=8), :]
                pool_stage[1, pl.ds(q, blocks, stride=8), :] = summed[x, y, z] * 0.125
                for i in range(2):
                    for j in range(2):
                        for l in range(2):
                            p = 16 * (2 * x + i) + 4 * (2 * y + j) + 2 * z + l
                            stage[p * blocks : (p + 1) * blocks, :] = g * slope[x, i, y, j, z, l]
    grad[core] = stage[...].astype(BF16)
    pooled_ref[...] = pool_stage[1].astype(BF16)
    gcopies = rim_copies(grad, glow, ghigh, gsend, grecv, me, core, n)
    for copy in gcopies:
        copy.start()
    fill_interior(tile_g, grad, occ, core, blocks)
    wait_peer(grad, gsend, grecv, me, core)
    fill_interior(tile_g, grad, occ, 1 - core, blocks)
    flipped = jnp.concatenate([grad[0], grad[1]], axis=1).T
    for one in sums:
        for k in range(one.k0, one.k1):
            total[k] = jnp.dot(
                flipped, window(tile_in, core, k // 9, k // 3 % 3, k % 3),
                preferred_element_type=F32,
            )
        one.start_sum(0)
    wait_rims(grad, glow, ghigh, gsend, grecv, me, core)
    fill_border(tile_g, glow, ghigh, pick, blocks)
    load_b.wait()
    acc = None
    for a in range(3):
        for e in range(3):
            left = jnp.concatenate(
                [window(tile_g, h, 2 - a, 2 - e, 2 - c) for c in range(3) for h in range(2)],
                axis=1,
            )
            k = 9 * a + 3 * e
            right = jnp.concatenate([wb[k + c] for c in range(3)], axis=1)
            term = lax.dot_general(
                left, right, (((1,), (1,)), ((), ())), preferred_element_type=F32
            )
            acc = term if acc is None else acc + term
    for p in range(64):
        stage[pl.ds(p, blocks, stride=64), :] = acc[p * blocks : (p + 1) * blocks]
    gf_ref[...] = stage[...].astype(BF16)
    for step in range(steps):
        for one in sums:
            one.end_sum(step)
            if step + 1 < steps:
                one.start_sum(step + 1)
            else:
                one.start_gather(0)
    gathers = len(sums[0].trail)
    for step in range(1, gathers + 1):
        for one in sums:
            one.end_gather()
            if step < gathers:
                one.start_gather(step)
    for copy in copies + gcopies:
        copy.wait_send()


def body(features, weight, neighbours, send_slots, grad_pooled):
    n = lax.axis_size("morton")
    blocks = features.shape[0]
    width = features.shape[-1]
    full = weight.shape[-1]
    slots = send_slots.shape[-1]
    lanes = jnp.arange(width, dtype=jnp.int32)
    column = jnp.where(neighbours > blocks, neighbours - 1, neighbours)
    column = jnp.where(neighbours > blocks + slots, column - slots, column)
    column = jnp.where(neighbours == blocks, -1, column)
    names = (column.T[:, :, None] == lanes).astype(F32)
    occ = jnp.broadcast_to((neighbours[:, 13] < blocks).astype(F32)[:, None], (blocks, width))
    places = jnp.where(send_slots[0] < blocks, send_slots[0] + blocks, -1)
    sel = (places[:, :, None] == lanes).astype(F32)
    rows = blocks * 64
    steps = len(bit_orders(n)[0])
    sizes = [max(full >> (step + 1), 16) for step in range(steps)]
    buffers = [pltpu.VMEM((27, size, width), BF16) for size in sizes]
    vmem = pl.BlockSpec(memory_space=pltpu.VMEM)
    pooled, gf, gw = pl.pallas_call(
        functools.partial(kernel, n),
        out_shape=(
            jax.ShapeDtypeStruct((blocks * 8, width), BF16),
            jax.ShapeDtypeStruct((rows, width), BF16),
            jax.ShapeDtypeStruct((27, full, width), BF16),
        ),
        in_specs=[vmem, pl.BlockSpec(memory_space=pl.ANY), vmem, vmem, vmem, vmem],
        out_specs=(vmem, vmem, vmem),
        scratch_shapes=[
            pltpu.VMEM((27, full, width), BF16),
            pltpu.VMEM((27, width, full), BF16),
            pltpu.VMEM((2, rows, width), BF16),
            pltpu.VMEM((2, rows // 4, width), BF16),
            pltpu.VMEM((2, rows // 4, width), BF16),
            pltpu.VMEM((2, rows, width), BF16),
            pltpu.VMEM((2, rows // 4, width), BF16),
            pltpu.VMEM((2, rows // 4, width), BF16),
            pltpu.VMEM((2, 6, 6, 6, blocks, width), F32),
            pltpu.VMEM((2, 6, 6, 6, blocks, width), F32),
            pltpu.VMEM((27, blocks, width), F32),
            pltpu.VMEM((2, slots, width), F32),
            pltpu.VMEM((rows, width), F32),
            pltpu.VMEM((2, blocks * 8, width), F32),
            pltpu.SemaphoreType.DMA((2,)),
            pltpu.SemaphoreType.DMA((5,)),
            pltpu.SemaphoreType.DMA((5,)),
            pltpu.SemaphoreType.DMA((5,)),
            pltpu.SemaphoreType.DMA((5,)),
            pltpu.SemaphoreType.DMA((2,)),
            pltpu.SemaphoreType.DMA((2,)),
            pltpu.VMEM((27, full, width), F32),
            pltpu.SemaphoreType.DMA((len(CUTS) - 1, 2 * steps, 2)),
        ]
        + buffers * 2,
        compiler_params=pltpu.CompilerParams(
            collective_id=0, has_side_effects=True, vmem_limit_bytes=48 * 1024 * 1024
        ),
    )(
        features.reshape(rows, width), weight, names, occ, sel,
        grad_pooled.reshape(blocks * 8, width),
    )
    return (
        pooled.reshape(grad_pooled.shape),
        gf.reshape(features.shape),
        jnp.swapaxes(gw, 1, 2).astype(F32),
    )


def solution(mesh):
    in_specs = (
        P("morton", None, None, None, "chan"),
        P(),
        P("morton", None),
        P("morton", None, None),
        P("morton", None, None, None, "chan"),
    )
    out_specs = (
        P("morton", None, None, None, "chan"),
        P("morton", None, None, None, "chan"),
        P(None, "chan", None),
    )
    return jax.shard_map(body, mesh=mesh, in_specs=in_specs, out_specs=out_specs, check_vma=False)
```

```python
import functools

import jax
import jax.numpy as jnp
from jax import lax
from jax.experimental import pallas as pl
from jax.experimental.pallas import tpu as pltpu
from jax.sharding import PartitionSpec as P

MESH = pl.DeviceIdType.MESH
F32 = jnp.float32
BF16 = jnp.bfloat16


def offsets_of(x):
    return ([-1] if x == 3 else []) + [0] + ([1] if x == 0 else [])


def place(offset, x):
    return 0 if offset < 0 else (5 if offset > 0 else x + 1)


def rim_copies(own, low, high, send, recv, me, core, n):
    nxt, prv = lax.rem(me + 1, n), lax.rem(me + n - 1, n)
    rows = own.shape[1]
    plane = rows // 4
    peer = 1 - core
    copies = [
        pltpu.make_async_remote_copy(
            src_ref=own.at[core], dst_ref=own.at[core], send_sem=send.at[0],
            recv_sem=recv.at[0], device_id=(me, peer), device_id_type=MESH,
        )
    ]
    for target in range(2):
        copies.append(
            pltpu.make_async_remote_copy(
                src_ref=own.at[core, pl.ds(rows - plane, plane)], dst_ref=low.at[core],
                send_sem=send.at[1 + target], recv_sem=recv.at[1 + core],
                device_id=(nxt, target), device_id_type=MESH,
            )
        )
        copies.append(
            pltpu.make_async_remote_copy(
                src_ref=own.at[core, pl.ds(0, plane)], dst_ref=high.at[core],
                send_sem=send.at[3 + target], recv_sem=recv.at[3 + core],
                device_id=(prv, target), device_id_type=MESH,
            )
        )
    return copies


def wait_peer(own, send, recv, me, core):
    pltpu.make_async_remote_copy(
        src_ref=own.at[1 - core], dst_ref=own.at[1 - core], send_sem=send.at[0],
        recv_sem=recv.at[0], device_id=(me, 1 - core), device_id_type=MESH,
    ).wait_recv()


def wait_rims(own, low, high, send, recv, me, core):
    for half in range(2):
        for ref, base in ((low, 1), (high, 3)):
            pltpu.make_async_remote_copy(
                src_ref=ref.at[half], dst_ref=ref.at[half], send_sem=send.at[0],
                recv_sem=recv.at[base + half], device_id=(me, 1 - core), device_id_type=MESH,
            ).wait_recv()


def fill_interior(tile, own, occ, half, blocks):
    value = own[half].astype(F32).reshape(4, 4, 4, blocks, own.shape[-1])
    tile[half, 1:5, 1:5, 1:5] = value * occ


def fill_border(tile, low, high, pick, blocks):
    width = low.shape[-1]
    for x in range(4):
        for y in range(4):
            for z in range(4):
                ks = [
                    (a, e, c)
                    for a in offsets_of(x)
                    for e in offsets_of(y)
                    for c in offsets_of(z)
                    if (a, e, c) != (0, 0, 0)
                ]
                if not ks:
                    continue
                left = jnp.concatenate(
                    [pick[9 * a + 3 * e + c + 13] for a, e, c in ks], axis=0
                )
                own = jnp.concatenate([tile[h, 1 + x, 1 + y, 1 + z] for h in range(2)], axis=1)
                if x in (0, 3):
                    rim = high if x == 0 else low
                    r = (4 * y + z) * blocks
                    other = jnp.concatenate(
                        [rim[h, r : r + blocks, :].astype(F32) for h in range(2)], axis=1
                    )
                    right = jnp.concatenate([own, other], axis=0)
                else:
                    right = own
                got = jnp.dot(
                    left[:, : right.shape[0]].astype(BF16), right.astype(BF16),
                    preferred_element_type=F32,
                )
                for j, (a, e, c) in enumerate(ks):
                    for h in range(2):
                        tile[h, place(a, x), place(e, y), place(c, z)] = got[
                            j * blocks : (j + 1) * blocks, h * width : (h + 1) * width
                        ]


def window(tile, half, a, e, c):
    part = tile[half, a : a + 4, e : e + 4, c : c + 4]
    return part.reshape(-1, part.shape[-1]).astype(BF16)


CUTS = (0, 5, 10, 14, 19, 24, 27)


def bit_orders(n):
    bits = []
    while 2 ** len(bits) < n:
        bits.append(2 ** len(bits))
    if len(bits) < 4:
        return (bits, bits[::-1], bits)
    x, y, near, far = bits[:4]
    return (bits, [y, near, far, x] + bits[4:], [near, x, y, far] + bits[4:])


class Summing:
    def __init__(self, piece, n, me, core, acc, out, sends, recvs, sem):
        self.k0, self.k1 = CUTS[piece], CUTS[piece + 1]
        self.piece, self.me, self.core = piece, me, core
        self.acc, self.out, self.sends, self.recvs = acc, out, sends, recvs
        self.sem = sem
        self.bits = bit_orders(n)[piece % 3]
        self.low, self.size = 0, acc.shape[1]
        self.trail, self.pending = [], None

    def partner(self, bit):
        mine = lax.rem(lax.div(self.me, bit), 2)
        return mine, self.me + bit * (1 - 2 * mine)

    def rows(self, low, size):
        if isinstance(low, int):
            return pl.ds(low, size)
        return pl.ds(pl.multiple_of(low, 16), size)

    def copy(self, step, src, dst, to):
        pair = self.sem.at[self.piece, step]
        return pltpu.make_async_remote_copy(
            src_ref=src, dst_ref=dst, send_sem=pair.at[0], recv_sem=pair.at[1],
            device_id=(to, self.core), device_id_type=MESH,
        )

    def start_sum(self, step):
        ks = pl.ds(self.k0, self.k1 - self.k0)
        mine, to = self.partner(self.bits[step])
        halves = self.size > 16
        part = self.size // 2 if halves else self.size
        gone = self.low + (1 - mine) * part if halves else self.low
        kept = self.low + mine * part if halves else self.low
        send = self.sends[step].at[ks]
        send[...] = self.acc[ks, self.rows(gone, part), :].astype(BF16)
        copy = self.copy(step, send, self.recvs[step].at[ks], to)
        copy.start()
        self.pending = copy
        self.trail.append((self.bits[step], halves, self.low, self.size))
        self.low, self.size = kept, part

    def end_sum(self, step):
        ks = pl.ds(self.k0, self.k1 - self.k0)
        self.pending.wait()
        rows = self.rows(self.low, self.size)
        own = self.acc[ks, rows, :]
        if not self.trail[-1][1]:
            own = self.sends[step][ks].astype(F32)
        total = own + self.recvs[step][ks].astype(F32)
        if step + 1 < len(self.bits):
            self.acc[ks, rows, :] = total
        else:
            self.out[ks, rows, :] = total.astype(BF16)
            self.trail = [t for t in self.trail if t[1]]

    def start_gather(self, step):
        bit, _, low, size = self.trail[-1 - step]
        ks = pl.ds(self.k0, self.k1 - self.k0)
        _, to = self.partner(bit)
        held = self.out.at[ks, self.rows(self.low, self.size)]
        copy = self.copy(len(self.bits) + step, held, held, to)
        copy.start()
        self.pending = copy
        self.low, self.size = low, size

    def end_gather(self):
        self.pending.wait()


def kernel(
    n, feat_ref, weight_ref, names_ref, occ_ref, sel_ref, gp_ref,
    pooled_ref, gf_ref, gw_ref,
    wf, wb, feat, flow, fhigh, grad, glow, ghigh, tile_in, tile_g, pick, merge,
    stage, pool_stage, wsem, fsend, frecv, gsend, grecv, ssend, srecv, total, rsem, *bufs,
):
    me, core = lax.axis_index("morton"), lax.axis_index("chan")
    nxt, prv = lax.rem(me + 1, n), lax.rem(me + n - 1, n)
    width = feat_ref.shape[-1]
    rows = feat_ref.shape[0]
    blocks = rows // 64
    columns = pl.ds(pl.multiple_of(core * width, width), width)
    load_f = pltpu.make_async_copy(weight_ref.at[:, :, columns], wf, wsem.at[0])
    load_b = pltpu.make_async_copy(weight_ref.at[:, columns, :], wb, wsem.at[1])
    load_f.start()
    load_b.start()
    barrier = pltpu.get_barrier_semaphore()
    steps = len(bufs) // 2
    sums = [
        Summing(i, n, me, core, total, gw_ref, bufs[:steps], bufs[steps:], rsem)
        for i in range(len(CUTS) - 1)
    ]
    others = [(sums[0].partner(bit)[1], core) for bit in sums[0].bits]
    for target in [(me, 1 - core), (nxt, 0), (nxt, 1), (prv, 0), (prv, 1)] + others:
        pl.semaphore_signal(barrier, inc=1, device_id=target, device_id_type=MESH)
    stage[...] = feat_ref[...].astype(F32)
    feat[core] = jnp.concatenate(
        [stage[pl.ds(p, blocks, stride=64), :] for p in range(64)], axis=0
    ).astype(BF16)
    pl.semaphore_wait(barrier, 5 + len(others))
    sels = [
        pltpu.make_async_remote_copy(
            src_ref=sel_ref.at[1], dst_ref=merge.at[0], send_sem=ssend.at[0],
            recv_sem=srecv.at[0], device_id=(nxt, core), device_id_type=MESH,
        ),
        pltpu.make_async_remote_copy(
            src_ref=sel_ref.at[0], dst_ref=merge.at[1], send_sem=ssend.at[1],
            recv_sem=srecv.at[1], device_id=(prv, core), device_id_type=MESH,
        ),
    ]
    copies = rim_copies(feat, flow, fhigh, fsend, frecv, me, core, n)
    for copy in sels + copies:
        copy.start()
    occ = occ_ref[...]
    fill_interior(tile_in, feat, occ, core, blocks)
    for copy in sels:
        copy.wait()
    eye = (
        lax.broadcasted_iota(jnp.int32, (blocks, width), 0)
        == lax.broadcasted_iota(jnp.int32, (blocks, width), 1)
    ).astype(F32)
    pick[0:9] = jnp.dot(
        names_ref[0:9].reshape(9 * blocks, width)[:, : 2 * blocks],
        jnp.concatenate([eye, merge[0]], axis=0), preferred_element_type=F32,
    ).reshape(9, blocks, width)
    pick[9:18] = names_ref[9:18]
    pick[18:27] = jnp.dot(
        names_ref[18:27].reshape(9 * blocks, width)[:, : 2 * blocks],
        jnp.concatenate([eye, merge[1]], axis=0), preferred_element_type=F32,
    ).reshape(9, blocks, width)
    wait_peer(feat, fsend, frecv, me, core)
    fill_interior(tile_in, feat, occ, 1 - core, blocks)
    wait_rims(feat, flow, fhigh, fsend, frecv, me, core)
    fill_border(tile_in, flow, fhigh, pick, blocks)
    load_f.wait()
    acc = None
    for a in range(3):
        for e in range(3):
            left = jnp.concatenate(
                [window(tile_in, h, a, e, c) for c in range(3) for h in range(2)], axis=1
            )
            k = 9 * a + 3 * e
            right = wf[k : k + 3].reshape(6 * width, width)
            term = jnp.dot(left, right, preferred_element_type=F32)
            acc = term if acc is None else acc + term
    s = jax.nn.sigmoid(acc)
    act = (acc * s).reshape(2, 2, 2, 2, 2, 2, blocks, width)
    summed = act[:, 0] + act[:, 1]
    summed = summed[:, :, 0] + summed[:, :, 1]
    summed = summed[:, :, :, 0] + summed[:, :, :, 1]
    slope = (s * (1.0 + acc * (1.0 - s))).reshape(2, 2, 2, 2, 2, 2, blocks, width)
    pool_stage[0] = gp_ref[...].astype(F32) * 0.125
    for x in range(2):
        for y in range(2):
            for z in range(2):
                q = 4 * x + 2 * y + z
                g = pool_stage[0, pl.ds(q, blocks, stride=8), :]
                pool_stage[1, pl.ds(q, blocks, stride=8), :] = summed[x, y, z] * 0.125
                for i in range(2):
                    for j in range(2):
                        for l in range(2):
                            p = 16 * (2 * x + i) + 4 * (2 * y + j) + 2 * z + l
                            stage[p * blocks : (p + 1) * blocks, :] = g * slope[x, i, y, j, z, l]
    grad[core] = stage[...].astype(BF16)
    pooled_ref[...] = pool_stage[1].astype(BF16)
    gcopies = rim_copies(grad, glow, ghigh, gsend, grecv, me, core, n)
    for copy in gcopies:
        copy.start()
    fill_interior(tile_g, grad, occ, core, blocks)
    wait_peer(grad, gsend, grecv, me, core)
    fill_interior(tile_g, grad, occ, 1 - core, blocks)
    flipped = jnp.concatenate([grad[0], grad[1]], axis=1).T
    for one in sums:
        for k in range(one.k0, one.k1):
            term = jnp.dot(
                flipped, window(tile_in, core, k // 9, k // 3 % 3, k % 3),
                preferred_element_type=F32,
            )
            for half in range(2):
                span = slice(half * width, (half + 1) * width)
                total[k, span] = term[span].T
        one.start_sum(0)
    wait_rims(grad, glow, ghigh, gsend, grecv, me, core)
    fill_border(tile_g, glow, ghigh, pick, blocks)
    load_b.wait()
    acc = None
    for a in range(3):
        for e in range(3):
            left = jnp.concatenate(
                [window(tile_g, h, 2 - a, 2 - e, 2 - c) for c in range(3) for h in range(2)],
                axis=1,
            )
            k = 9 * a + 3 * e
            right = jnp.concatenate([wb[k + c] for c in range(3)], axis=1)
            term = lax.dot_general(
                left, right, (((1,), (1,)), ((), ())), preferred_element_type=F32
            )
            acc = term if acc is None else acc + term
    for p in range(64):
        stage[pl.ds(p, blocks, stride=64), :] = acc[p * blocks : (p + 1) * blocks]
    gf_ref[...] = stage[...].astype(BF16)
    for step in range(steps):
        for one in sums:
            one.end_sum(step)
            if step + 1 < steps:
                one.start_sum(step + 1)
            else:
                one.start_gather(0)
    gathers = len(sums[0].trail)
    for step in range(1, gathers + 1):
        for one in sums:
            one.end_gather()
            if step < gathers:
                one.start_gather(step)
    for copy in copies + gcopies:
        copy.wait_send()


def body(features, weight, neighbours, send_slots, grad_pooled):
    n = lax.axis_size("morton")
    blocks = features.shape[0]
    width = features.shape[-1]
    full = weight.shape[-1]
    slots = send_slots.shape[-1]
    lanes = jnp.arange(width, dtype=jnp.int32)
    column = jnp.where(neighbours > blocks, neighbours - 1, neighbours)
    column = jnp.where(neighbours > blocks + slots, column - slots, column)
    column = jnp.where(neighbours == blocks, -1, column)
    names = (column.T[:, :, None] == lanes).astype(F32)
    occ = jnp.broadcast_to((neighbours[:, 13] < blocks).astype(F32)[:, None], (blocks, width))
    places = jnp.where(send_slots[0] < blocks, send_slots[0] + blocks, -1)
    sel = (places[:, :, None] == lanes).astype(F32)
    rows = blocks * 64
    steps = len(bit_orders(n)[0])
    sizes = [max(full >> (step + 1), 16) for step in range(steps)]
    buffers = [pltpu.VMEM((27, size, width), BF16) for size in sizes]
    vmem = pl.BlockSpec(memory_space=pltpu.VMEM)
    pooled, gf, gw = pl.pallas_call(
        functools.partial(kernel, n),
        out_shape=(
            jax.ShapeDtypeStruct((blocks * 8, width), BF16),
            jax.ShapeDtypeStruct((rows, width), BF16),
            jax.ShapeDtypeStruct((27, full, width), BF16),
        ),
        in_specs=[vmem, pl.BlockSpec(memory_space=pl.ANY), vmem, vmem, vmem, vmem],
        out_specs=(vmem, vmem, vmem),
        scratch_shapes=[
            pltpu.VMEM((27, full, width), BF16),
            pltpu.VMEM((27, width, full), BF16),
            pltpu.VMEM((2, rows, width), BF16),
            pltpu.VMEM((2, rows // 4, width), BF16),
            pltpu.VMEM((2, rows // 4, width), BF16),
            pltpu.VMEM((2, rows, width), BF16),
            pltpu.VMEM((2, rows // 4, width), BF16),
            pltpu.VMEM((2, rows // 4, width), BF16),
            pltpu.VMEM((2, 6, 6, 6, blocks, width), F32),
            pltpu.VMEM((2, 6, 6, 6, blocks, width), F32),
            pltpu.VMEM((27, blocks, width), F32),
            pltpu.VMEM((2, slots, width), F32),
            pltpu.VMEM((rows, width), F32),
            pltpu.VMEM((2, blocks * 8, width), F32),
            pltpu.SemaphoreType.DMA((2,)),
            pltpu.SemaphoreType.DMA((5,)),
            pltpu.SemaphoreType.DMA((5,)),
            pltpu.SemaphoreType.DMA((5,)),
            pltpu.SemaphoreType.DMA((5,)),
            pltpu.SemaphoreType.DMA((2,)),
            pltpu.SemaphoreType.DMA((2,)),
            pltpu.VMEM((27, full, width), F32),
            pltpu.SemaphoreType.DMA((len(CUTS) - 1, 2 * steps, 2)),
        ]
        + buffers * 2,
        compiler_params=pltpu.CompilerParams(
            collective_id=0, has_side_effects=True, vmem_limit_bytes=60 * 1024 * 1024
        ),
    )(
        features.reshape(rows, width), weight, names, occ, sel,
        grad_pooled.reshape(blocks * 8, width),
    )
    return (
        pooled.reshape(grad_pooled.shape),
        gf.reshape(features.shape),
        jnp.swapaxes(gw.reshape(27, 2, width, width), 1, 2).reshape(27, width, full).astype(F32),
    )


def solution(mesh):
    in_specs = (
        P("morton", None, None, None, "chan"),
        P(),
        P("morton", None),
        P("morton", None, None),
        P("morton", None, None, None, "chan"),
    )
    out_specs = (
        P("morton", None, None, None, "chan"),
        P("morton", None, None, None, "chan"),
        P(None, "chan", None),
    )
    return jax.shard_map(body, mesh=mesh, in_specs=in_specs, out_specs=out_specs, check_vma=False)
```

```python
import functools

import jax
import jax.numpy as jnp
from jax import lax
from jax.experimental import pallas as pl
from jax.experimental.pallas import tpu as pltpu
from jax.sharding import PartitionSpec as P

MESH = pl.DeviceIdType.MESH
F32 = jnp.float32
BF16 = jnp.bfloat16


def offsets_of(x):
    return ([-1] if x == 3 else []) + [0] + ([1] if x == 0 else [])


def place(offset, x):
    return 0 if offset < 0 else (5 if offset > 0 else x + 1)


def rim_copies(own, low, high, send, recv, me, core, n):
    nxt, prv = lax.rem(me + 1, n), lax.rem(me + n - 1, n)
    rows = own.shape[1]
    plane = rows // 4
    peer = 1 - core
    copies = [
        pltpu.make_async_remote_copy(
            src_ref=own.at[core], dst_ref=own.at[core], send_sem=send.at[0],
            recv_sem=recv.at[0], device_id=(me, peer), device_id_type=MESH,
        )
    ]
    for target in range(2):
        copies.append(
            pltpu.make_async_remote_copy(
                src_ref=own.at[core, pl.ds(rows - plane, plane)], dst_ref=low.at[core],
                send_sem=send.at[1 + target], recv_sem=recv.at[1 + core],
                device_id=(nxt, target), device_id_type=MESH,
            )
        )
        copies.append(
            pltpu.make_async_remote_copy(
                src_ref=own.at[core, pl.ds(0, plane)], dst_ref=high.at[core],
                send_sem=send.at[3 + target], recv_sem=recv.at[3 + core],
                device_id=(prv, target), device_id_type=MESH,
            )
        )
    return copies


def wait_peer(own, send, recv, me, core):
    pltpu.make_async_remote_copy(
        src_ref=own.at[1 - core], dst_ref=own.at[1 - core], send_sem=send.at[0],
        recv_sem=recv.at[0], device_id=(me, 1 - core), device_id_type=MESH,
    ).wait_recv()


def wait_rims(own, low, high, send, recv, me, core):
    for half in range(2):
        for ref, base in ((low, 1), (high, 3)):
            pltpu.make_async_remote_copy(
                src_ref=ref.at[half], dst_ref=ref.at[half], send_sem=send.at[0],
                recv_sem=recv.at[base + half], device_id=(me, 1 - core), device_id_type=MESH,
            ).wait_recv()


def fill_interior(tile, own, occ, half, blocks):
    value = own[half].astype(F32).reshape(4, 4, 4, blocks, own.shape[-1])
    tile[half, 1:5, 1:5, 1:5] = value * occ


def fill_border(tile, low, high, pick, blocks):
    width = low.shape[-1]
    for x in range(4):
        for y in range(4):
            for z in range(4):
                ks = [
                    (a, e, c)
                    for a in offsets_of(x)
                    for e in offsets_of(y)
                    for c in offsets_of(z)
                    if (a, e, c) != (0, 0, 0)
                ]
                if not ks:
                    continue
                left = jnp.concatenate(
                    [pick[9 * a + 3 * e + c + 13] for a, e, c in ks], axis=0
                )
                own = jnp.concatenate([tile[h, 1 + x, 1 + y, 1 + z] for h in range(2)], axis=1)
                if x in (0, 3):
                    rim = high if x == 0 else low
                    r = (4 * y + z) * blocks
                    other = jnp.concatenate(
                        [rim[h, r : r + blocks, :].astype(F32) for h in range(2)], axis=1
                    )
                    right = jnp.concatenate([own, other], axis=0)
                else:
                    right = own
                got = jnp.dot(
                    left[:, : right.shape[0]].astype(BF16), right.astype(BF16),
                    preferred_element_type=F32,
                )
                for j, (a, e, c) in enumerate(ks):
                    for h in range(2):
                        tile[h, place(a, x), place(e, y), place(c, z)] = got[
                            j * blocks : (j + 1) * blocks, h * width : (h + 1) * width
                        ]


def window(tile, half, a, e, c):
    part = tile[half, a : a + 4, e : e + 4, c : c + 4]
    return part.reshape(-1, part.shape[-1]).astype(BF16)


CUTS = (0, 5, 10, 14, 19, 24, 27)


def bit_orders(n):
    bits = []
    while 2 ** len(bits) < n:
        bits.append(2 ** len(bits))
    if len(bits) < 4:
        return (bits, bits[::-1], bits)
    x, y, near, far = bits[:4]
    return (bits, [y, near, far, x] + bits[4:], [near, x, y, far] + bits[4:])


class Summing:
    def __init__(self, piece, n, me, core, acc, out, sends, recvs, sem):
        self.k0, self.k1 = CUTS[piece], CUTS[piece + 1]
        self.piece, self.me, self.core = piece, me, core
        self.acc, self.out, self.sends, self.recvs = acc, out, sends, recvs
        self.sem = sem
        self.bits = bit_orders(n)[piece % 3]
        self.low, self.size = 0, acc.shape[1]
        self.trail, self.pending = [], None

    def partner(self, bit):
        mine = lax.rem(lax.div(self.me, bit), 2)
        return mine, self.me + bit * (1 - 2 * mine)

    def rows(self, low, size):
        if isinstance(low, int):
            return pl.ds(low, size)
        return pl.ds(pl.multiple_of(low, 16), size)

    def copy(self, step, src, dst, to):
        pair = self.sem.at[self.piece, step]
        return pltpu.make_async_remote_copy(
            src_ref=src, dst_ref=dst, send_sem=pair.at[0], recv_sem=pair.at[1],
            device_id=(to, self.core), device_id_type=MESH,
        )

    def start_sum(self, step):
        ks = pl.ds(self.k0, self.k1 - self.k0)
        mine, to = self.partner(self.bits[step])
        halves = self.size > 16
        part = self.size // 2 if halves else self.size
        gone = self.low + (1 - mine) * part if halves else self.low
        kept = self.low + mine * part if halves else self.low
        send = self.sends[step].at[ks]
        send[...] = self.acc[ks, self.rows(gone, part), :].astype(BF16)
        copy = self.copy(step, send, self.recvs[step].at[ks], to)
        copy.start()
        self.pending = copy
        self.trail.append((self.bits[step], halves, self.low, self.size))
        self.low, self.size = kept, part

    def end_sum(self, step):
        ks = pl.ds(self.k0, self.k1 - self.k0)
        self.pending.wait()
        rows = self.rows(self.low, self.size)
        own = self.acc[ks, rows, :]
        if not self.trail[-1][1]:
            own = self.sends[step][ks].astype(F32)
        total = own + self.recvs[step][ks].astype(F32)
        if step + 1 < len(self.bits):
            self.acc[ks, rows, :] = total
        else:
            self.out[ks, rows, :] = total.astype(BF16)
            self.trail = [t for t in self.trail if t[1]]

    def start_gather(self, step):
        bit, _, low, size = self.trail[-1 - step]
        ks = pl.ds(self.k0, self.k1 - self.k0)
        _, to = self.partner(bit)
        held = self.out.at[ks, self.rows(self.low, self.size)]
        copy = self.copy(len(self.bits) + step, held, held, to)
        copy.start()
        self.pending = copy
        self.low, self.size = low, size

    def end_gather(self):
        self.pending.wait()


def kernel(
    n, feat_ref, weight_ref, near_ref, slots_ref, gp_ref,
    pooled_ref, gf_ref, gw_ref,
    wf, wb, feat, flow, fhigh, grad, glow, ghigh, tile_in, tile_g, pick, sel, merge,
    stage, pool_stage, wsem, fsend, frecv, gsend, grecv, ssend, srecv, total, rsem, *bufs,
):
    me, core = lax.axis_index("morton"), lax.axis_index("chan")
    nxt, prv = lax.rem(me + 1, n), lax.rem(me + n - 1, n)
    width = feat_ref.shape[-1]
    rows = feat_ref.shape[0]
    blocks = rows // 64
    columns = pl.ds(pl.multiple_of(core * width, width), width)
    load_f = pltpu.make_async_copy(weight_ref.at[:, :, columns], wf, wsem.at[0])
    load_b = pltpu.make_async_copy(weight_ref.at[:, columns, :], wb, wsem.at[1])
    load_f.start()
    load_b.start()
    barrier = pltpu.get_barrier_semaphore()
    steps = len(bufs) // 2
    sums = [
        Summing(i, n, me, core, total, gw_ref, bufs[:steps], bufs[steps:], rsem)
        for i in range(len(CUTS) - 1)
    ]
    others = [(sums[0].partner(bit)[1], core) for bit in sums[0].bits]
    for target in [(me, 1 - core), (nxt, 0), (nxt, 1), (prv, 0), (prv, 1)] + others:
        pl.semaphore_signal(barrier, inc=1, device_id=target, device_id_type=MESH)
    lane = lax.broadcasted_iota(jnp.int32, (2 * blocks, width), 1)
    row = lax.broadcasted_iota(jnp.int32, (2 * blocks, width), 0)
    slots = slots_ref.shape[-1]
    for side in range(2):
        hit = row == lane - slots
        for j in range(slots):
            named = slots_ref[0, side, j]
            hit = hit | ((lane == j) & (row == named + blocks) & (named < blocks))
        sel[side] = jnp.where(hit, 1.0, 0.0).astype(F32)
    near = near_ref[...]
    mark = lane[:blocks]
    for k in range(27):
        name = jnp.broadcast_to(near[:, k : k + 1], (blocks, width))
        if k // 9 != 1:
            rim = jnp.where(name > blocks + slots, name - slots, name) - (blocks + 1)
            name = jnp.where(name < blocks, name + slots, jnp.where(name == blocks, -1, rim))
        else:
            name = jnp.where(name < blocks, name, -1)
        pick[k] = jnp.where(mark == name, 1.0, 0.0).astype(F32)
    occ = jnp.where(jnp.broadcast_to(near[:, 13:14], (blocks, width)) < blocks, 1.0, 0.0)
    stage[...] = feat_ref[...].astype(F32)
    feat[core] = jnp.concatenate(
        [stage[pl.ds(p, blocks, stride=64), :] for p in range(64)], axis=0
    ).astype(BF16)
    pl.semaphore_wait(barrier, 5 + len(others))
    sels = [
        pltpu.make_async_remote_copy(
            src_ref=sel.at[1], dst_ref=merge.at[0], send_sem=ssend.at[0],
            recv_sem=srecv.at[0], device_id=(nxt, core), device_id_type=MESH,
        ),
        pltpu.make_async_remote_copy(
            src_ref=sel.at[0], dst_ref=merge.at[1], send_sem=ssend.at[1],
            recv_sem=srecv.at[1], device_id=(prv, core), device_id_type=MESH,
        ),
    ]
    copies = rim_copies(feat, flow, fhigh, fsend, frecv, me, core, n)
    for copy in sels + copies:
        copy.start()
    fill_interior(tile_in, feat, occ, core, blocks)
    for copy in sels:
        copy.wait()
    for side in range(2):
        ks = slice(18 * side, 18 * side + 9)
        named = pick[ks].reshape(9 * blocks, width)
        spread = lax.dot_general(
            named, merge[side], (((1,), (1,)), ((), ())), preferred_element_type=F32
        )
        pick[ks, :, : 2 * blocks] = spread.reshape(9, blocks, 2 * blocks)
    wait_peer(feat, fsend, frecv, me, core)
    fill_interior(tile_in, feat, occ, 1 - core, blocks)
    wait_rims(feat, flow, fhigh, fsend, frecv, me, core)
    fill_border(tile_in, flow, fhigh, pick, blocks)
    load_f.wait()
    acc = None
    for a in range(3):
        for e in range(3):
            left = jnp.concatenate(
                [window(tile_in, h, a, e, c) for c in range(3) for h in range(2)], axis=1
            )
            k = 9 * a + 3 * e
            right = wf[k : k + 3].reshape(6 * width, width)
            term = jnp.dot(left, right, preferred_element_type=F32)
            acc = term if acc is None else acc + term
    s = jax.nn.sigmoid(acc)
    act = (acc * s).reshape(2, 2, 2, 2, 2, 2, blocks, width)
    summed = act[:, 0] + act[:, 1]
    summed = summed[:, :, 0] + summed[:, :, 1]
    summed = summed[:, :, :, 0] + summed[:, :, :, 1]
    slope = (s * (1.0 + acc * (1.0 - s))).reshape(2, 2, 2, 2, 2, 2, blocks, width)
    pool_stage[0] = gp_ref[...].astype(F32) * 0.125
    for x in range(2):
        for y in range(2):
            for z in range(2):
                q = 4 * x + 2 * y + z
                g = pool_stage[0, pl.ds(q, blocks, stride=8), :]
                pool_stage[1, pl.ds(q, blocks, stride=8), :] = summed[x, y, z] * 0.125
                for i in range(2):
                    for j in range(2):
                        for l in range(2):
                            p = 16 * (2 * x + i) + 4 * (2 * y + j) + 2 * z + l
                            stage[p * blocks : (p + 1) * blocks, :] = g * slope[x, i, y, j, z, l]
    grad[core] = stage[...].astype(BF16)
    pooled_ref[...] = pool_stage[1].astype(BF16)
    gcopies = rim_copies(grad, glow, ghigh, gsend, grecv, me, core, n)
    for copy in gcopies:
        copy.start()
    fill_interior(tile_g, grad, occ, core, blocks)
    wait_peer(grad, gsend, grecv, me, core)
    fill_interior(tile_g, grad, occ, 1 - core, blocks)
    flipped = jnp.concatenate([grad[0], grad[1]], axis=1).T
    for one in sums:
        for k in range(one.k0, one.k1):
            term = jnp.dot(
                flipped, window(tile_in, core, k // 9, k // 3 % 3, k % 3),
                preferred_element_type=F32,
            )
            for half in range(2):
                span = slice(half * width, (half + 1) * width)
                total[k, span] = term[span].T
        one.start_sum(0)
    wait_rims(grad, glow, ghigh, gsend, grecv, me, core)
    fill_border(tile_g, glow, ghigh, pick, blocks)
    load_b.wait()
    acc = None
    for a in range(3):
        for e in range(3):
            left = jnp.concatenate(
                [window(tile_g, h, 2 - a, 2 - e, 2 - c) for c in range(3) for h in range(2)],
                axis=1,
            )
            k = 9 * a + 3 * e
            right = jnp.concatenate([wb[k + c] for c in range(3)], axis=1)
            term = lax.dot_general(
                left, right, (((1,), (1,)), ((), ())), preferred_element_type=F32
            )
            acc = term if acc is None else acc + term
    for p in range(64):
        stage[pl.ds(p, blocks, stride=64), :] = acc[p * blocks : (p + 1) * blocks]
    gf_ref[...] = stage[...].astype(BF16)
    for step in range(steps):
        for one in sums:
            one.end_sum(step)
            if step + 1 < steps:
                one.start_sum(step + 1)
            else:
                one.start_gather(0)
    gathers = len(sums[0].trail)
    for step in range(1, gathers + 1):
        for one in sums:
            one.end_gather()
            if step < gathers:
                one.start_gather(step)
    for copy in copies + gcopies:
        copy.wait_send()


def body(features, weight, neighbours, send_slots, grad_pooled):
    n = lax.axis_size("morton")
    blocks = features.shape[0]
    width = features.shape[-1]
    full = weight.shape[-1]
    rows = blocks * 64
    steps = len(bit_orders(n)[0])
    sizes = [max(full >> (step + 1), 16) for step in range(steps)]
    buffers = [pltpu.VMEM((27, size, width), BF16) for size in sizes]
    vmem = pl.BlockSpec(memory_space=pltpu.VMEM)
    pooled, gf, gw = pl.pallas_call(
        functools.partial(kernel, n),
        out_shape=(
            jax.ShapeDtypeStruct((blocks * 8, width), BF16),
            jax.ShapeDtypeStruct((rows, width), BF16),
            jax.ShapeDtypeStruct((27, full, width), BF16),
        ),
        in_specs=[
            vmem,
            pl.BlockSpec(memory_space=pl.ANY),
            vmem,
            pl.BlockSpec(memory_space=pltpu.SMEM),
            vmem,
        ],
        out_specs=(vmem, vmem, vmem),
        scratch_shapes=[
            pltpu.VMEM((27, full, width), BF16),
            pltpu.VMEM((27, width, full), BF16),
            pltpu.VMEM((2, rows, width), BF16),
            pltpu.VMEM((2, rows // 4, width), BF16),
            pltpu.VMEM((2, rows // 4, width), BF16),
            pltpu.VMEM((2, rows, width), BF16),
            pltpu.VMEM((2, rows // 4, width), BF16),
            pltpu.VMEM((2, rows // 4, width), BF16),
            pltpu.VMEM((2, 6, 6, 6, blocks, width), F32),
            pltpu.VMEM((2, 6, 6, 6, blocks, width), F32),
            pltpu.VMEM((27, blocks, width), F32),
            pltpu.VMEM((2, 2 * blocks, width), F32),
            pltpu.VMEM((2, 2 * blocks, width), F32),
            pltpu.VMEM((rows, width), F32),
            pltpu.VMEM((2, blocks * 8, width), F32),
            pltpu.SemaphoreType.DMA((2,)),
            pltpu.SemaphoreType.DMA((5,)),
            pltpu.SemaphoreType.DMA((5,)),
            pltpu.SemaphoreType.DMA((5,)),
            pltpu.SemaphoreType.DMA((5,)),
            pltpu.SemaphoreType.DMA((2,)),
            pltpu.SemaphoreType.DMA((2,)),
            pltpu.VMEM((27, full, width), F32),
            pltpu.SemaphoreType.DMA((len(CUTS) - 1, 2 * steps, 2)),
        ]
        + buffers * 2,
        compiler_params=pltpu.CompilerParams(
            collective_id=0, has_side_effects=True, vmem_limit_bytes=60 * 1024 * 1024
        ),
    )(
        features.reshape(rows, width), weight, neighbours, send_slots,
        grad_pooled.reshape(blocks * 8, width),
    )
    return (
        pooled.reshape(grad_pooled.shape),
        gf.reshape(features.shape),
        jnp.swapaxes(gw.reshape(27, 2, width, width), 1, 2).reshape(27, width, full).astype(F32),
    )


def solution(mesh):
    in_specs = (
        P("morton", None, None, None, "chan"),
        P(),
        P("morton", None),
        P("morton", None, None),
        P("morton", None, None, None, "chan"),
    )
    out_specs = (
        P("morton", None, None, None, "chan"),
        P("morton", None, None, None, "chan"),
        P(None, "chan", None),
    )
    return jax.shard_map(body, mesh=mesh, in_specs=in_specs, out_specs=out_specs, check_vma=False)
```
